32 devices in a mesh: segment: 16 (over z, y, core), expert: 2 (over x).
Axes of the slice: x: 2, y: 2, z: 4, core: 2. Of those that a mesh axis runs over, the one named last changes fastest.
Arguments:
- grad_in: bfloat16 [256, 3072], P('expert'), may hold values from -6 to 6
- route_b: int32 [256, 2], P('expert'), may hold values from 0 to 1, as said below
- prob_b: float32 [256, 2], P('expert'), may hold values from 0.1 to 1
- pre_act: bfloat16 [2, 2, 256, 8192], P('expert', None, None, 'segment'), may hold values from -6 to 6
- saved_in: bfloat16 [256, 3072], P('expert'), may hold values from -6 to 6
- grad_saved: bfloat16 [256, 3072], P('expert'), may hold values from -4 to 4
- route_c: int32 [256, 2], P('expert'), may hold values from 0 to 1, as said below
- prob_c: float32 [256, 2], P('expert'), may hold values from 0.1 to 1
- w_gate_up: bfloat16 [2, 2, 8192, 3072], P('expert', None, 'segment'), may hold values from -0.109375 to 0.109375
- w_down: bfloat16 [2, 8192, 3072], P('expert', 'segment'), may hold values from -0.0625 to 0.0625
Outputs:
- grad_out: bfloat16 [256, 3072], P('expert')
- grad_gate_up: bfloat16 [2, 2, 8192, 3072], P('expert', None, 'segment')
- grad_down: bfloat16 [2, 8192, 3072], P('expert', 'segment')
The draws below stay inside these ranges and needn't reach their ends.
Inputs may be any that keep to these rules, and one draw needn't show every extreme that they name: `route_b`: within each aligned block of 128 tokens the two experts of a token differ, one expert is named by exactly 128 tokens and none by more. `route_c`: within each aligned block of 128 tokens the two experts of a token differ, one expert is named by exactly 128 tokens and none by more.
All inputs are finite; a program needn't handle non-finite values.
Results may differ from the reference program's by a relative error of at most 0.0095.
Values may be sent and summed in bfloat16 or wider, within the bound.
A program may use at most 128 MiB of HBM per device.

```python
import math
import jax
import jax.numpy as jnp
from jax import lax

D = 3072
HID = 8192
TOK_DEV = 128
EXPERTS = 2
GROUPS = 16
TOKENS = 256
CAP = 128


def routing_block(key):
    key_order, key_names = jax.random.split(key)
    ordering = jax.random.permutation(key_order, TOK_DEV)
    expert_names = jax.random.permutation(key_names, EXPERTS)
    ranking = jnp.arange(TOK_DEV)
    column = ranking % EXPERTS
    group_id = ranking // EXPERTS
    hot_groups = TOK_DEV // (4 * EXPERTS)
    first_pick = expert_names[column]
    regular = expert_names[(column + 1 + group_id % (EXPERTS - 1)) % EXPERTS]
    early_pick = jnp.where(column == 0, expert_names[1 + group_id % (EXPERTS - 1)], expert_names[0])
    second_pick = jnp.where(group_id < hot_groups, early_pick, regular)
    pair_rows = jnp.stack([first_pick, second_pick], -1)
    inverse = jnp.argsort(ordering)
    return pair_rows[inverse].astype(jnp.int32)


def routing(key):
    block_keys = jax.random.split(key, EXPERTS)
    chosen = jax.vmap(routing_block)(block_keys)
    return chosen.reshape(TOKENS, 2)


def draw_route_b(key, part):
    return routing(jax.random.fold_in(key, 11))


def draw_route_c(key, part):
    return routing(jax.random.fold_in(key, 23))


def shard_levels(rng, extent, pieces, smallest, high):
    factor_of, own = 1.0, jax.random.fold_in(rng, 6)
    for dim, parts in pieces:
        heights = jnp.exp(jax.random.uniform(jax.random.fold_in(own, dim), (parts,), jnp.float32, smallest / len(pieces), high / len(pieces)))
        factor_of = factor_of * jnp.repeat(heights, extent[dim] // parts).reshape([-1 if axis == dim else 1 for axis in range(len(extent))])
    return factor_of


def gaussian(own_key, extent, spread, bound, pieces=(), held_as=jnp.bfloat16):
    level = shard_levels(own_key, extent, pieces, -0.22, 0.18) if pieces else 1.0
    values = jax.random.normal(own_key, extent, jnp.float32) * spread * level
    return jnp.minimum(jnp.maximum(values, -bound), bound).astype(held_as)


def setup_inputs(seed: int = 0) -> dict:
    keys = jax.random.split(jax.random.key(seed), 11)
    return {
        "grad_in": gaussian(keys[0], (TOKENS, D), 1.0, 6.0, ((0, 2),)),
        "route_b": draw_route_b(jax.random.fold_in(keys[10], 71), 0),
        "prob_b": jnp.clip(jnp.exp(math.log(1.0) - 2.3025851 * jax.random.uniform(keys[2], (TOKENS, 2), jnp.float32) ** shard_levels(keys[2], (TOKENS, 2), ((0, 2),), -0.2, 0.2)), 0.1, 1.0),
        "pre_act": gaussian(keys[3], (EXPERTS, 2, EXPERTS * CAP, HID), 1.0, 6.0, ((0, 2), (3, 16))),
        "saved_in": gaussian(keys[4], (TOKENS, D), 1.0, 6.0, ((0, 2),)),
        "grad_saved": gaussian(keys[5], (TOKENS, D), 0.3, 4.0, ((0, 2),)),
        "route_c": draw_route_c(jax.random.fold_in(keys[10], 71), 0),
        "prob_c": jnp.clip(jnp.exp(math.log(1.0) - 2.3025851 * jax.random.uniform(keys[7], (TOKENS, 2), jnp.float32) ** shard_levels(keys[7], (TOKENS, 2), ((0, 2),), -0.2, 0.2)), 0.1, 1.0),
        "w_gate_up": gaussian(keys[8], (EXPERTS, 2, HID, D), D ** -0.5, 0.109375, ((0, 2), (2, 16))),
        "w_down": gaussian(keys[9], (EXPERTS, HID, D), HID ** -0.5, 0.0625, ((0, 2), (1, 16))),
    }


def silu_parts(preact):
    sigmoid_val = jax.nn.sigmoid(preact)
    return preact * sigmoid_val, sigmoid_val * (1.0 + preact * (1.0 - sigmoid_val))


def settle(values):
    return lax.optimization_barrier(values.astype(jnp.bfloat16)).astype(jnp.float32)


def slot_ranks(routes):
    flat = routes.reshape(EXPERTS, 2 * TOK_DEV)
    onehot = (flat[:, :, None] == jnp.arange(EXPERTS, dtype=jnp.int32)[None, None, :]).astype(jnp.int32)
    before = jnp.cumsum(onehot, axis=1) - onehot
    ranks = jnp.sum(before * onehot, axis=2).astype(jnp.int32)
    return ranks.reshape(TOKENS, 2)


def fill_rows(values, routes, slots, scales):
    source = (jnp.arange(TOKENS) // TOK_DEV).astype(jnp.int32)
    buffer = jnp.zeros((EXPERTS, EXPERTS * CAP, D), jnp.float32)
    for which_k in range(2):
        picked = values.astype(jnp.float32) * scales[:, which_k][:, None]
        buffer = buffer.at[routes[:, which_k], source * CAP + slots[:, which_k]].set(picked)
    return settle(buffer)


def expert_input(items):
    sent_rows, stored, w_joint, w_last = items
    grad_act = jnp.dot(sent_rows, w_last.astype(jnp.float32).T)
    gate_pre = stored[0].astype(jnp.float32)
    upper_pre = stored[1].astype(jnp.float32)
    activated, slope_val = silu_parts(gate_pre)
    grad_gate = settle(grad_act * upper_pre * slope_val)
    grad_up = settle(grad_act * activated)
    group_width = HID // GROUPS
    w_first = w_joint[0].astype(jnp.float32)
    w_second = w_joint[1].astype(jnp.float32)

    def add_group(group, total):
        start = (group * group_width).astype(jnp.int32)
        part_gate = lax.dynamic_slice_in_dim(grad_gate, start, group_width, 1)
        part_up = lax.dynamic_slice_in_dim(grad_up, start, group_width, 1)
        rows_first = lax.dynamic_slice_in_dim(w_first, start, group_width, 0)
        rows_second = lax.dynamic_slice_in_dim(w_second, start, group_width, 0)
        partial_sum = jnp.dot(part_gate, rows_first) + jnp.dot(part_up, rows_second)
        return total + settle(partial_sum)

    initial = jnp.zeros((sent_rows.shape[0], D), jnp.float32)
    returned = lax.fori_loop(0, GROUPS, add_group, initial)
    return settle(returned)


def expert_weight(items):
    sent_rows, out_rows, w_joint, w_last = items
    gate_pre = jnp.dot(sent_rows, w_joint[0].astype(jnp.float32).T)
    upper_pre = jnp.dot(sent_rows, w_joint[1].astype(jnp.float32).T)
    activated, slope_val = silu_parts(gate_pre)
    hidden = settle(activated * upper_pre)
    grad_act = jnp.dot(out_rows, w_last.astype(jnp.float32).T)
    grad_gate = settle(grad_act * upper_pre * slope_val)
    grad_up = settle(grad_act * activated)
    grad_first = jnp.dot(grad_gate.T, sent_rows)
    grad_second = jnp.dot(grad_up.T, sent_rows)
    grad_joint = jnp.stack([grad_first, grad_second], axis=0).astype(jnp.bfloat16)
    grad_last = jnp.dot(hidden.T, out_rows).astype(jnp.bfloat16)
    return grad_joint, grad_last


def reference(grad_in, route_b, prob_b, pre_act, saved_in, grad_saved, route_c, prob_c, w_gate_up, w_down):
    source = (jnp.arange(TOKENS) // TOK_DEV).astype(jnp.int32)
    slot_b = slot_ranks(route_b)
    slot_c = slot_ranks(route_c)
    sent_b = fill_rows(grad_in, route_b, slot_b, prob_b)
    returned = lax.map(expert_input, (sent_b, pre_act, w_gate_up, w_down))
    summed = grad_in.astype(jnp.float32)
    for which_k in range(2):
        summed = summed + returned[route_b[:, which_k], source * CAP + slot_b[:, which_k]]
    grad_out = summed.astype(jnp.bfloat16)
    rows_c = fill_rows(saved_in, route_c, slot_c, jnp.ones((TOKENS, 2), jnp.float32))
    outs_c = fill_rows(grad_saved, route_c, slot_c, prob_c)
    grad_joint, grad_last = lax.map(expert_weight, (rows_c, outs_c, w_gate_up, w_down))
    return grad_out, grad_joint, grad_last
```

```python
import functools

import jax
import jax.numpy as jnp
from jax import lax
from jax.experimental import pallas as pl
from jax.experimental.pallas import tpu as pltpu
from jax.sharding import PartitionSpec as P


def silu_parts(preact):
    sigmoid_val = jax.nn.sigmoid(preact)
    return (preact * sigmoid_val, sigmoid_val * (1.0 + preact * (1.0 - sigmoid_val)))


def slot_ranks(routes, experts):
    flat = routes.reshape(-1)
    onehot = (flat[:, None] == jnp.arange(experts, dtype=jnp.int32)[None, :]).astype(jnp.int32)
    before = jnp.cumsum(onehot, axis=0) - onehot
    ranks = jnp.sum(before * onehot, axis=1)
    return ranks.reshape(routes.shape[0], 2)


def slot_tables(routes, slots, probs, rows_total, per_expert):
    token_count = routes.shape[0]
    target = (routes * per_expert + slots).reshape(-1)
    slot_grid = jnp.arange(rows_total, dtype=jnp.int32)
    matches = (slot_grid[:, None] == target[None, :]).astype(jnp.int32)
    token_ids = jnp.repeat(jnp.arange(token_count, dtype=jnp.int32), 2)
    token_index = jnp.sum(matches * token_ids[None, :], axis=1)
    filled = jnp.sum(matches, axis=1).astype(jnp.float32)
    slot_scale = jnp.sum(matches.astype(jnp.float32) * probs.reshape(-1)[None, :], axis=1)
    return (token_index, filled, slot_scale)


def gather_rows(values, token_index, weight):
    picked = jnp.take(values, token_index, axis=0).astype(jnp.float32) * weight[:, None]
    return picked.astype(jnp.bfloat16)


def contract_last(left, right):
    return lax.dot_general(
        left, right, (((1,), (1,)), ((), ())), preferred_element_type=jnp.float32
    )


def contract_first(left, right):
    return lax.dot_general(
        left, right, (((0,), (0,)), ((), ())), preferred_element_type=jnp.float32
    )


def add_picked(base, returned, positions):
    summed = base.astype(jnp.float32)
    summed = summed + jnp.take(returned, positions[:, 0], axis=0).astype(jnp.float32)
    summed = summed + jnp.take(returned, positions[:, 1], axis=0).astype(jnp.float32)
    return summed.astype(jnp.bfloat16)


def body(
    grad_in, route_b, prob_b, pre_act, saved_in, grad_saved, route_c, prob_c, w_gate_up, w_down
):
    experts = lax.axis_size("expert")
    rows_total = pre_act.shape[2]
    per_expert = rows_total // experts
    model_width = grad_in.shape[1]
    hidden_units = w_down.shape[1]
    joined = w_gate_up.reshape(2 * hidden_units, model_width)
    w_last = w_down.reshape(hidden_units, model_width)
    stored = pre_act.reshape(2, rows_total, hidden_units)
    slot_b = slot_ranks(route_b, experts)
    slot_c = slot_ranks(route_c, experts)
    index_b, filled_b, scale_b = slot_tables(route_b, slot_b, prob_b, rows_total, per_expert)
    sent_b = gather_rows(grad_in, index_b, scale_b).reshape(experts, per_expert, model_width)
    index_c, filled_c, scale_c = slot_tables(route_c, slot_c, prob_c, rows_total, per_expert)
    rows_c = gather_rows(saved_in, index_c, filled_c).reshape(experts, per_expert, model_width)
    outs_c = gather_rows(grad_saved, index_c, scale_c).reshape(experts, per_expert, model_width)
    arrived_b = lax.all_to_all(sent_b, "expert", split_axis=0, concat_axis=0, tiled=True).reshape(
        rows_total, model_width
    )
    grad_act = contract_last(arrived_b, w_last)
    gate_pre = stored[0].astype(jnp.float32)
    upper_pre = stored[1].astype(jnp.float32)
    activated, slope_val = silu_parts(gate_pre)
    grad_gate = (grad_act * upper_pre * slope_val).astype(jnp.bfloat16)
    grad_up = (grad_act * activated).astype(jnp.bfloat16)
    grad_pair = jnp.concatenate([grad_gate, grad_up], axis=1)
    expert_side = jnp.dot(grad_pair, joined, preferred_element_type=jnp.float32)
    positions = route_b * per_expert + slot_b
    sections = lax.axis_size("segment")
    width_part = model_width // sections
    shares = lax.psum_scatter(
        expert_side.astype(jnp.bfloat16), "segment", scatter_dimension=1, tiled=True
    )
    returned = lax.all_to_all(
        shares.reshape(experts, per_expert, width_part),
        "expert",
        split_axis=0,
        concat_axis=0,
        tiled=True,
    )
    returned = returned.reshape(rows_total, width_part)
    start = lax.axis_index("segment") * width_part
    column_in = lax.dynamic_slice_in_dim(grad_in, start, width_part, 1)
    segment_cols = add_picked(column_in, returned, positions)
    grad_out = lax.all_gather(segment_cols, "segment", axis=1, tiled=True)
    arrived_rows, arrived_outs = (
        lax.all_to_all(rows_c, "expert", split_axis=0, concat_axis=0, tiled=True),
        lax.all_to_all(outs_c, "expert", split_axis=0, concat_axis=0, tiled=True),
    )
    sent_rows = arrived_rows.reshape(rows_total, model_width)
    out_rows = arrived_outs.reshape(rows_total, model_width)
    pre_both = contract_last(sent_rows, joined)
    gate_c = pre_both[:, :hidden_units]
    upper_c = pre_both[:, hidden_units:]
    active_c, slope_c = silu_parts(gate_c)
    hidden = (active_c * upper_c).astype(jnp.bfloat16)
    grad_act_c = contract_last(out_rows, w_last)
    grad_gate_c = (grad_act_c * upper_c * slope_c).astype(jnp.bfloat16)
    grad_up_c = (grad_act_c * active_c).astype(jnp.bfloat16)
    pair_c = jnp.concatenate([grad_gate_c, grad_up_c], axis=1)
    grad_joined = contract_first(pair_c, sent_rows).astype(jnp.bfloat16)
    grad_last = contract_first(hidden, out_rows).astype(jnp.bfloat16)
    grad_gate_up = grad_joined.reshape(1, 2, hidden_units, model_width)
    grad_down = grad_last.reshape(1, hidden_units, model_width)
    return (grad_out, grad_gate_up, grad_down)


MESH = pl.DeviceIdType.MESH
BF16 = jnp.bfloat16
F32 = jnp.float32


def exchange_kernel(
    zn, gin, sin, gsv, rb, pb, rc, pc, pre, wgu, wd,
    gout, rows_o, outs_o, gt_o,
    tok, wv, prev, wsend, wrecv, ps, pr, pf, pm, r2a, r2b, s3a, s3b, r3a, r3b, qf, qs, r4, go, gt,
    send_sem, recv_sem, local_sem,
):
    s = lax.axis_index("segment")
    x = lax.axis_index("expert")
    c, y, z = s % 2, (s // 2) % 2, s // 4
    T, D = gin.shape
    H = wd.shape[0]
    half, part = D // 2, D // 4
    yrows, zrows, quarter = T // 2, T // 2 // zn, T // 4
    piece = quarter // 2
    sib = {"segment": s + 1 - 2 * c, "expert": x}
    ypal = {"segment": s + 2 - 4 * y, "expert": x}
    xpal = {"segment": s, "expert": 1 - x}
    zpal = [None] + [{"segment": ((z + k) % zn) * 4 + s % 4, "expert": x} for k in range(1, zn)]

    used = [0, 0]
    sent = []

    def remote(src, dst, to):
        i = used[0]
        used[0] += 1
        return pltpu.make_async_remote_copy(
            src_ref=src, dst_ref=dst, send_sem=send_sem.at[i], recv_sem=recv_sem.at[i],
            device_id=to, device_id_type=MESH,
        )

    def start(copy):
        copy.start()
        sent.append(copy)
        return copy

    def local(src, dst):
        i = used[1]
        used[1] += 1
        copy = pltpu.make_async_copy(src, dst, local_sem.at[i])
        copy.start()
        return copy

    in_b = local(gin, tok.at[0, pl.ds(0, T)])
    in_wd = local(wd, wv.at[pl.ds(2 * H, H)])
    in_pre = local(pre, prev)
    in_wgu = local(wgu, wv.at[pl.ds(0, 2 * H)])
    in_rows = local(sin, tok.at[1, pl.ds(0, T)])
    in_outs = local(gsv, tok.at[2, pl.ds(0, T)])

    barrier = pltpu.get_barrier_semaphore()
    pals = [sib, ypal, xpal] + zpal[1:]
    for pal in pals:
        pl.semaphore_signal(barrier, inc=1, device_id=pal, device_id_type=MESH)
    pl.semaphore_wait(barrier, len(pals))

    def at_rows(a, q, h, base):
        return tok.at[a, pl.ds(pl.multiple_of(base + q * quarter + h * piece, 16), piece)]

    q_me = 2 * y + c
    q_y = 2 * (1 - y) + c
    arrays = (gin, sin, gsv)
    by_x, by_y, by_sib = {}, {}, {}
    for a in range(3):
        for h in range(2):
            src = arrays[a].at[pl.ds(pl.multiple_of(q_me * quarter + h * piece, 16), piece)]
            by_x[a, h] = remote(src, at_rows(a, q_me, h, T), xpal)
            by_y[a, h] = remote(at_rows(a, q_me, h, T), at_rows(a, q_me, h, T), ypal)
            by_sib[a, h, 0] = remote(at_rows(a, q_me, h, T), at_rows(a, q_me, h, T), sib)
            by_sib[a, h, 1] = remote(at_rows(a, q_y, h, T), at_rows(a, q_y, h, T), sib)

    def send_x(a):
        for h in range(2):
            start(by_x[a, h])

    def pass_x(a):
        for h in range(2):
            by_x[a, h].wait_recv()
            start(by_y[a, h])
            start(by_sib[a, h, 0])

    def pass_y(a):
        for h in range(2):
            by_y[a, h].wait_recv()
            start(by_sib[a, h, 1])

    def wait_sib(a):
        for h in range(2):
            for i in range(2):
                by_sib[a, h, i].wait_recv()

    send_x(0)

    def share(routes, probs, expert):
        picked = jnp.where(routes[...] == expert, probs[...], 0.0)
        return picked[0:1] + picked[1:2]

    wsend[...] = jnp.zeros_like(wsend)
    wsend[0:1, :] = share(rb, pb, 1 - x)
    wsend[1:2, :] = share(rc, pc, 1 - x)
    weights = start(remote(wsend, wrecv, xpal))

    def nt(left, right):
        return lax.dot_general(left, right, (((1,), (1,)), ((), ())), preferred_element_type=F32)

    def column(row):
        return jnp.broadcast_to(row, (T, T)).T[:, 0:1]

    def hidden_b(first, scale, block):
        act = nt(tok[0, first:first + T, :], wv[2 * H:3 * H, :]) * scale
        rows = pl.ds(pl.multiple_of(block * T, T), T)
        gate = prev[0, rows, :].astype(F32)
        upper = prev[1, rows, :].astype(F32)
        activated, slope = silu_parts(gate)
        return (act * upper * slope).astype(BF16), (act * activated).astype(BF16)

    tile = part

    def back_b(pair, first, core, put):
        for n in range(half // tile):
            cols = pl.ds(pl.multiple_of(core * half + n * tile, 128), tile)
            total = jnp.dot(pair[0], wv[0:H, cols], preferred_element_type=F32)
            total = total + jnp.dot(pair[1], wv[H:2 * H, cols], preferred_element_type=F32)
            put(slice(first, first + T), slice(n * tile, n * tile + tile), total)

    def put_send(rows, cols, total):
        ps[rows, cols] = total.astype(BF16)

    def put_keep(rows, cols, total):
        pf[rows, cols] = total

    in_b.wait()
    in_wd.wait()
    in_pre.wait()
    pair_own = hidden_b(0, column(share(rb, pb, x)), x)
    pass_x(0)
    send_x(1)
    in_wgu.wait()
    back_b(pair_own, 0, 1 - c, put_send)
    to_sib = [remote(ps.at[pl.ds(i * T, T)], pr.at[pl.ds(i * T, T)], sib) for i in range(2)]
    start(to_sib[0])
    pass_y(0)
    back_b(pair_own, 0, c, put_keep)
    weights.wait_recv()
    wait_sib(0)
    pair_other = hidden_b(T, column(wrecv[0:1, :]), 1 - x)
    back_b(pair_other, T, 1 - c, put_send)
    start(to_sib[1])
    pass_x(1)
    back_b(pair_other, T, c, put_keep)

    mine = pl.multiple_of(y * yrows, 16)
    theirs = pl.multiple_of((1 - y) * yrows, 16)
    lo, hi = slice(0, part), slice(part, half)
    to_sib[0].wait_recv()
    pf[0:T, :] = pf[0:T, :] + pr[0:T, :].astype(F32)
    pm[0:T, :] = pf[0:T, :].astype(BF16)
    s2b0 = start(remote(pm.at[pl.ds(theirs, yrows), pl.ds(part, part)], r2b.at[pl.ds(0, yrows)], ypal))
    to_sib[1].wait_recv()
    pf[T:2 * T, :] = pf[T:2 * T, :] + pr[T:2 * T, :].astype(F32)
    pm[T:2 * T, :] = pf[T:2 * T, :].astype(BF16)
    s2a = start(remote(pm.at[pl.ds(T, T), pl.ds(0, part)], r2a, xpal))
    s2b1 = start(remote(pm.at[pl.ds(T + theirs, yrows), pl.ds(part, part)], r2b.at[pl.ds(yrows, yrows)], ypal))

    pass_y(1)
    in_rows.wait()
    wait_sib(1)
    out_rows = local(tok.at[1], rows_o)
    for i in range(2 * H // 256):
        units = slice(i * 256, i * 256 + 256)
        gt[units, :] = nt(wv[units, :], tok[1])

    s2a.wait_recv()
    s3a[...] = (pf[pl.ds(theirs, yrows), lo] + r2a[pl.ds(theirs, yrows), :].astype(F32)).astype(BF16)
    c3a = start(remote(s3a, r3a, ypal))
    s2b1.wait_recv()
    s3b[...] = (pf[pl.ds(T + mine, yrows), hi] + r2b[yrows:2 * yrows, :].astype(F32)).astype(BF16)
    c3b = start(remote(s3b, r3b, xpal))
    s2b0.wait_recv()
    qf[:, lo] = pf[pl.ds(mine, yrows), lo] + r2a[pl.ds(mine, yrows), :].astype(F32)
    qf[:, hi] = pf[pl.ds(mine, yrows), hi] + r2b[0:yrows, :].astype(F32)
    c3a.wait_recv()
    qf[:, lo] = qf[:, lo] + r3a[...].astype(F32)
    c3b.wait_recv()
    qf[:, hi] = qf[:, hi] + r3b[...].astype(F32)
    qs[...] = qf[...].astype(BF16)
    z_sums = []
    for k in range(1, zn):
        there = pl.ds(pl.multiple_of(((z + k) % zn) * zrows, 16), zrows)
        z_sums.append(start(remote(qs.at[there], r4.at[k - 1], zpal[k])))
    send_x(2)
    here = pl.multiple_of(z * zrows, 16)
    cols_me = pl.ds(pl.multiple_of(c * half, 128), half)
    chunk = qf[pl.ds(here, zrows), :] + tok[0, pl.ds(mine + here, zrows), cols_me].astype(F32)
    for k in range(1, zn):
        z_sums[k - 1].wait_recv()
        chunk = chunk + r4[k - 1].astype(F32)
    go[pl.ds(mine + here, zrows), cols_me] = chunk.astype(BF16)

    def finished(yy, k):
        return go.at[pl.ds(pl.multiple_of(yy * yrows + ((z + zn - k) % zn) * zrows, 16), zrows), cols_me]

    z_out = [None] + [start(remote(finished(y, 0), finished(y, 0), zpal[k])) for k in range(1, zn)]
    y_out, sib_out = [], []
    y_out.append(start(remote(finished(y, 0), finished(y, 0), ypal)))
    sib_out.append(start(remote(finished(y, 0), finished(y, 0), sib)))
    pass_x(2)
    for k in range(1, zn):
        z_out[k].wait_recv()
        y_out.append(start(remote(finished(y, k), finished(y, k), ypal)))
        sib_out.append(start(remote(finished(y, k), finished(y, k), sib)))
    pass_y(2)
    in_outs.wait()
    wait_sib(2)
    out_outs = local(tok.at[2], outs_o)
    scale_own = share(rc, pc, x)
    scale_c = jnp.concatenate([scale_own, wrecv[1:2, :]], axis=1)
    gtb = gt_o
    for i in range(H // 256):
        units = slice(i * 256, i * 256 + 256)
        uppers = slice(H + i * 256, H + i * 256 + 256)
        downs = slice(2 * H + i * 256, 2 * H + i * 256 + 256)
        act = nt(wv[downs, :], tok[2]) * scale_c
        upper = gt[uppers, :]
        activated, slope = silu_parts(gt[units, :])
        gtb[units, :] = (act * upper * slope).astype(BF16)
        gtb[uppers, :] = (act * activated).astype(BF16)
        gtb[downs, :] = (activated * upper * scale_c).astype(BF16)
    for k in range(zn):
        y_out[k].wait_recv()
        sib_out.append(start(remote(finished(1 - y, k), finished(1 - y, k), sib)))
    for copy in sib_out:
        copy.wait_recv()
    out_go = local(go, gout)
    for copy in sent:
        copy.wait_send()
    out_rows.wait()
    out_outs.wait()
    out_go.wait()


def weight_kernel(joined_steps, gt, rows, outs, gin, joint, last, gout):
    i = pl.program_id(0)

    @pl.when(i == 0)
    def _():
        gout[...] = gin[...]

    @pl.when(i < joined_steps)
    def _():
        joint[...] = jnp.dot(gt[...], rows[...], preferred_element_type=F32).astype(BF16)

    @pl.when(i >= joined_steps)
    def _():
        last[...] = jnp.dot(gt[...], outs[...], preferred_element_type=F32).astype(BF16)


def dense_body(
    grad_in, route_b, prob_b, pre_act, saved_in, grad_saved, route_c, prob_c, w_gate_up, w_down
):
    sections = lax.axis_size("segment")
    zn = sections // 4
    T, D = grad_in.shape
    H = w_down.shape[1]
    half, part = D // 2, D // 4
    copies = 24 + 1 + 2 + 3 + 2 + 2 * (zn - 1) + 3 * zn
    hbm = pl.BlockSpec(memory_space=pl.ANY)
    vmem = pl.BlockSpec(memory_space=pltpu.VMEM)
    gout, rows, outs, gt = pl.pallas_call(
        functools.partial(exchange_kernel, zn),
        out_shape=(
            jax.ShapeDtypeStruct((T, D), BF16),
            jax.ShapeDtypeStruct((2 * T, D), BF16),
            jax.ShapeDtypeStruct((2 * T, D), BF16),
            jax.ShapeDtypeStruct((3 * H, 2 * T), BF16),
        ),
        in_specs=[hbm] * 3 + [vmem] * 4 + [hbm] * 3,
        out_specs=(hbm, hbm, hbm, vmem),
        scratch_shapes=[
            pltpu.VMEM((3, 2 * T, D), BF16),
            pltpu.VMEM((3 * H, D), BF16),
            pltpu.VMEM((2, 2 * T, H), BF16),
            pltpu.VMEM((8, T), F32),
            pltpu.VMEM((8, T), F32),
            pltpu.VMEM((2 * T, half), BF16),
            pltpu.VMEM((2 * T, half), BF16),
            pltpu.VMEM((2 * T, half), F32),
            pltpu.VMEM((2 * T, half), BF16),
            pltpu.VMEM((T, part), BF16),
            pltpu.VMEM((T, part), BF16),
            pltpu.VMEM((T // 2, part), BF16),
            pltpu.VMEM((T // 2, part), BF16),
            pltpu.VMEM((T // 2, part), BF16),
            pltpu.VMEM((T // 2, part), BF16),
            pltpu.VMEM((T // 2, half), F32),
            pltpu.VMEM((T // 2, half), BF16),
            pltpu.VMEM((zn - 1, T // 2 // zn, half), BF16),
            pltpu.VMEM((T, D), BF16),
            pltpu.VMEM((2 * H, 2 * T), F32),
            pltpu.SemaphoreType.DMA((copies,)),
            pltpu.SemaphoreType.DMA((copies,)),
            pltpu.SemaphoreType.DMA((9,)),
        ],
        compiler_params=pltpu.CompilerParams(
            collective_id=0, has_side_effects=True, vmem_limit_bytes=56 * 1024 * 1024
        ),
        name="exchange",
    )(
        grad_in, saved_in, grad_saved, route_b.T, prob_b.T, route_c.T, prob_c.T,
        pre_act.reshape(2, 2 * T, H), w_gate_up.reshape(2 * H, D), w_down.reshape(H, D),
    )
    rows_step = 256
    joined_steps, last_steps = 2 * H // rows_step, H // rows_step
    whole = pl.BlockSpec((2 * T, D), lambda i: (0, 0))
    one = pl.BlockSpec((T, D), lambda i: (0, 0))
    joint, last, grad_out = pl.pallas_call(
        functools.partial(weight_kernel, joined_steps),
        grid=(joined_steps + last_steps,),
        out_shape=(
            jax.ShapeDtypeStruct((2 * H, D), BF16),
            jax.ShapeDtypeStruct((H, D), BF16),
            jax.ShapeDtypeStruct((T, D), BF16),
        ),
        in_specs=[pl.BlockSpec((rows_step, 2 * T), lambda i: (i, 0)), whole, whole, one],
        out_specs=(
            pl.BlockSpec((rows_step, D), lambda i: (jnp.minimum(i, joined_steps - 1), 0)),
            pl.BlockSpec((rows_step, D), lambda i: (jnp.maximum(i - joined_steps, 0), 0)),
            one,
        ),
        compiler_params=pltpu.CompilerParams(vmem_limit_bytes=48 * 1024 * 1024),
        name="weights",
    )(gt, rows, outs, gout)
    return grad_out, joint.reshape(1, 2, H, D), last.reshape(1, H, D)


def dense_fits(mesh):
    return mesh.shape["expert"] == 2 and mesh.shape["segment"] == 16


def solution(mesh):
    in_specs = (
        P("expert", None),
        P("expert", None),
        P("expert", None),
        P("expert", None, None, "segment"),
        P("expert", None),
        P("expert", None),
        P("expert", None),
        P("expert", None),
        P("expert", None, "segment", None),
        P("expert", "segment", None),
    )
    out_specs = (
        P("expert", None),
        P("expert", None, "segment", None),
        P("expert", "segment", None),
    )
    chosen = dense_body if dense_fits(mesh) else body
    return jax.shard_map(chosen, mesh=mesh, in_specs=in_specs, out_specs=out_specs, check_vma=False)
```

```python
import functools

import jax
import jax.numpy as jnp
from jax import lax
from jax.experimental import pallas as pl
from jax.experimental.pallas import tpu as pltpu
from jax.sharding import PartitionSpec as P


def silu_parts(preact):
    sigmoid_val = jax.nn.sigmoid(preact)
    return (preact * sigmoid_val, sigmoid_val * (1.0 + preact * (1.0 - sigmoid_val)))


def slot_ranks(routes, experts):
    flat = routes.reshape(-1)
    onehot = (flat[:, None] == jnp.arange(experts, dtype=jnp.int32)[None, :]).astype(jnp.int32)
    before = jnp.cumsum(onehot, axis=0) - onehot
    ranks = jnp.sum(before * onehot, axis=1)
    return ranks.reshape(routes.shape[0], 2)


def slot_tables(routes, slots, probs, rows_total, per_expert):
    token_count = routes.shape[0]
    target = (routes * per_expert + slots).reshape(-1)
    slot_grid = jnp.arange(rows_total, dtype=jnp.int32)
    matches = (slot_grid[:, None] == target[None, :]).astype(jnp.int32)
    token_ids = jnp.repeat(jnp.arange(token_count, dtype=jnp.int32), 2)
    token_index = jnp.sum(matches * token_ids[None, :], axis=1)
    filled = jnp.sum(matches, axis=1).astype(jnp.float32)
    slot_scale = jnp.sum(matches.astype(jnp.float32) * probs.reshape(-1)[None, :], axis=1)
    return (token_index, filled, slot_scale)


def gather_rows(values, token_index, weight):
    picked = jnp.take(values, token_index, axis=0).astype(jnp.float32) * weight[:, None]
    return picked.astype(jnp.bfloat16)


def contract_last(left, right):
    return lax.dot_general(
        left, right, (((1,), (1,)), ((), ())), preferred_element_type=jnp.float32
    )


def contract_first(left, right):
    return lax.dot_general(
        left, right, (((0,), (0,)), ((), ())), preferred_element_type=jnp.float32
    )


def add_picked(base, returned, positions):
    summed = base.astype(jnp.float32)
    summed = summed + jnp.take(returned, positions[:, 0], axis=0).astype(jnp.float32)
    summed = summed + jnp.take(returned, positions[:, 1], axis=0).astype(jnp.float32)
    return summed.astype(jnp.bfloat16)


def body(
    grad_in, route_b, prob_b, pre_act, saved_in, grad_saved, route_c, prob_c, w_gate_up, w_down
):
    experts = lax.axis_size("expert")
    rows_total = pre_act.shape[2]
    per_expert = rows_total // experts
    model_width = grad_in.shape[1]
    hidden_units = w_down.shape[1]
    joined = w_gate_up.reshape(2 * hidden_units, model_width)
    w_last = w_down.reshape(hidden_units, model_width)
    stored = pre_act.reshape(2, rows_total, hidden_units)
    slot_b = slot_ranks(route_b, experts)
    slot_c = slot_ranks(route_c, experts)
    index_b, filled_b, scale_b = slot_tables(route_b, slot_b, prob_b, rows_total, per_expert)
    sent_b = gather_rows(grad_in, index_b, scale_b).reshape(experts, per_expert, model_width)
    index_c, filled_c, scale_c = slot_tables(route_c, slot_c, prob_c, rows_total, per_expert)
    rows_c = gather_rows(saved_in, index_c, filled_c).reshape(experts, per_expert, model_width)
    outs_c = gather_rows(grad_saved, index_c, scale_c).reshape(experts, per_expert, model_width)
    arrived_b = lax.all_to_all(sent_b, "expert", split_axis=0, concat_axis=0, tiled=True).reshape(
        rows_total, model_width
    )
    grad_act = contract_last(arrived_b, w_last)
    gate_pre = stored[0].astype(jnp.float32)
    upper_pre = stored[1].astype(jnp.float32)
    activated, slope_val = silu_parts(gate_pre)
    grad_gate = (grad_act * upper_pre * slope_val).astype(jnp.bfloat16)
    grad_up = (grad_act * activated).astype(jnp.bfloat16)
    grad_pair = jnp.concatenate([grad_gate, grad_up], axis=1)
    expert_side = jnp.dot(grad_pair, joined, preferred_element_type=jnp.float32)
    positions = route_b * per_expert + slot_b
    sections = lax.axis_size("segment")
    width_part = model_width // sections
    shares = lax.psum_scatter(
        expert_side.astype(jnp.bfloat16), "segment", scatter_dimension=1, tiled=True
    )
    returned = lax.all_to_all(
        shares.reshape(experts, per_expert, width_part),
        "expert",
        split_axis=0,
        concat_axis=0,
        tiled=True,
    )
    returned = returned.reshape(rows_total, width_part)
    start = lax.axis_index("segment") * width_part
    column_in = lax.dynamic_slice_in_dim(grad_in, start, width_part, 1)
    segment_cols = add_picked(column_in, returned, positions)
    grad_out = lax.all_gather(segment_cols, "segment", axis=1, tiled=True)
    arrived_rows, arrived_outs = (
        lax.all_to_all(rows_c, "expert", split_axis=0, concat_axis=0, tiled=True),
        lax.all_to_all(outs_c, "expert", split_axis=0, concat_axis=0, tiled=True),
    )
    sent_rows = arrived_rows.reshape(rows_total, model_width)
    out_rows = arrived_outs.reshape(rows_total, model_width)
    pre_both = contract_last(sent_rows, joined)
    gate_c = pre_both[:, :hidden_units]
    upper_c = pre_both[:, hidden_units:]
    active_c, slope_c = silu_parts(gate_c)
    hidden = (active_c * upper_c).astype(jnp.bfloat16)
    grad_act_c = contract_last(out_rows, w_last)
    grad_gate_c = (grad_act_c * upper_c * slope_c).astype(jnp.bfloat16)
    grad_up_c = (grad_act_c * active_c).astype(jnp.bfloat16)
    pair_c = jnp.concatenate([grad_gate_c, grad_up_c], axis=1)
    grad_joined = contract_first(pair_c, sent_rows).astype(jnp.bfloat16)
    grad_last = contract_first(hidden, out_rows).astype(jnp.bfloat16)
    grad_gate_up = grad_joined.reshape(1, 2, hidden_units, model_width)
    grad_down = grad_last.reshape(1, hidden_units, model_width)
    return (grad_out, grad_gate_up, grad_down)


MESH = pl.DeviceIdType.MESH
BF16 = jnp.bfloat16
F32 = jnp.float32


def exchange_kernel(
    zn, gin, sin, gsv, rb, pb, rc, pc, pre, wgu, wd,
    gout, rows_o, outs_o, gt_o,
    tok, wv, prev, wsend, wrecv, ps, pr, pf, pm, r2a, r2b, s3a, s3b, r3a, r3b, qf, qs, r4, go, gt,
    send_sem, recv_sem, local_sem,
):
    s = lax.axis_index("segment")
    x = lax.axis_index("expert")
    c, y, z = s % 2, (s // 2) % 2, s // 4
    T, D = gin.shape
    H = wd.shape[0]
    half, part = D // 2, D // 4
    yrows, zrows, quarter = T // 2, T // 2 // zn, T // 4
    piece = quarter // 2
    sib = {"segment": s + 1 - 2 * c, "expert": x}
    ypal = {"segment": s + 2 - 4 * y, "expert": x}
    xpal = {"segment": s, "expert": 1 - x}
    zpal = [None] + [{"segment": ((z + k) % zn) * 4 + s % 4, "expert": x} for k in range(1, zn)]

    used = [0, 0]
    sent = []

    def remote(src, dst, to):
        i = used[0]
        used[0] += 1
        return pltpu.make_async_remote_copy(
            src_ref=src, dst_ref=dst, send_sem=send_sem.at[i], recv_sem=recv_sem.at[i],
            device_id=to, device_id_type=MESH,
        )

    def start(copy):
        copy.start()
        sent.append(copy)
        return copy

    def local(src, dst):
        i = used[1]
        used[1] += 1
        copy = pltpu.make_async_copy(src, dst, local_sem.at[i])
        copy.start()
        return copy

    def weight_rows(src, first, count):
        return [
            local(src.at[pl.ds(i * count, count)], wv.at[pl.ds(first + i * count, count)])
            for i in range(src.shape[0] // count)
        ]

    in_b = local(gin, tok.at[0, pl.ds(0, T)])
    in_wd = weight_rows(wd, 2 * H, H // 4)
    in_pre = local(pre, prev)

    barrier = pltpu.get_barrier_semaphore()
    pals = [sib, ypal, xpal] + zpal[1:]
    for pal in pals:
        pl.semaphore_signal(barrier, inc=1, device_id=pal, device_id_type=MESH)
    pl.semaphore_wait(barrier, len(pals))

    def at_rows(a, q, h, base):
        return tok.at[a, pl.ds(pl.multiple_of(base + q * quarter + h * piece, 16), piece)]

    zbit = z % 2
    znear = {"segment": s + 4 - 8 * zbit, "expert": x}
    arrays = (gin, sin, gsv)
    by_x, by_y, by_sib = {}, {}, {}
    for a in range(3):
        bit, pal = (zbit, znear) if a == 1 else (y, ypal)
        q_me, q_y = 2 * bit + c, 2 * (1 - bit) + c
        for h in range(2):
            src = arrays[a].at[pl.ds(pl.multiple_of(q_me * quarter + h * piece, 16), piece)]
            by_x[a, h] = remote(src, at_rows(a, q_me, h, T), xpal)
            by_y[a, h] = remote(at_rows(a, q_me, h, T), at_rows(a, q_me, h, T), pal)
            by_sib[a, h, 0] = remote(at_rows(a, q_me, h, T), at_rows(a, q_me, h, T), sib)
            by_sib[a, h, 1] = remote(at_rows(a, q_y, h, T), at_rows(a, q_y, h, T), sib)

    def send_x(a):
        for h in range(2):
            start(by_x[a, h])

    def pass_x(a, pieces=(0, 1)):
        for h in pieces:
            by_x[a, h].wait_recv()
            start(by_y[a, h])
            start(by_sib[a, h, 0])

    def pass_y(a):
        for h in range(2):
            by_y[a, h].wait_recv()
            start(by_sib[a, h, 1])

    def wait_sib(a):
        for h in range(2):
            for i in range(2):
                by_sib[a, h, i].wait_recv()

    send_x(0)

    def share(routes, probs, expert):
        picked = jnp.where(routes[...] == expert, probs[...], 0.0)
        return picked[0:1] + picked[1:2]

    wsend[...] = jnp.zeros_like(wsend)
    wsend[0:1, :] = share(rb, pb, 1 - x)
    wsend[1:2, :] = share(rc, pc, 1 - x)
    weights = start(remote(wsend, wrecv, xpal))

    in_wgu = weight_rows(wgu, 0, H // 4)

    def nt(left, right):
        return lax.dot_general(left, right, (((1,), (1,)), ((), ())), preferred_element_type=F32)

    def column(row):
        return jnp.broadcast_to(row, (T, T)).T[:, 0:1]

    def hidden_b(first, scale, block):
        act = nt(tok[0, first:first + T, :], wv[2 * H:3 * H, :]) * scale
        rows = pl.ds(pl.multiple_of(block * T, T), T)
        gate = prev[0, rows, :].astype(F32)
        upper = prev[1, rows, :].astype(F32)
        activated, slope = silu_parts(gate)
        return (act * upper * slope).astype(BF16), (act * activated).astype(BF16)

    tile = part

    def back_b(pair, first, core, put):
        for n in range(half // tile):
            cols = pl.ds(pl.multiple_of(core * half + n * tile, 128), tile)
            total = jnp.dot(pair[0], wv[0:H, cols], preferred_element_type=F32)
            total = total + jnp.dot(pair[1], wv[H:2 * H, cols], preferred_element_type=F32)
            put(slice(first, first + T), slice(n * tile, n * tile + tile), total)

    def put_send(rows, cols, total):
        ps[rows, cols] = total.astype(BF16)

    def put_keep(rows, cols, total):
        pf[rows, cols] = total

    def wait_all(copies):
        for copy in copies:
            copy.wait()

    pass_x(0, (0,))
    wait_all([in_b, in_pre] + in_wd)
    pair_own = hidden_b(0, column(share(rb, pb, x)), x)
    pass_x(0, (1,))
    send_x(1)
    wait_all(in_wgu)
    in_rows = local(sin, tok.at[1, pl.ds(0, T)])
    in_outs = local(gsv, tok.at[2, pl.ds(0, T)])
    back_b(pair_own, 0, 1 - c, put_send)
    to_sib = [remote(ps.at[pl.ds(i * T, T)], pr.at[pl.ds(i * T, T)], sib) for i in range(2)]
    start(to_sib[0])
    pass_y(0)
    back_b(pair_own, 0, c, put_keep)
    pass_x(1)

    mine = pl.multiple_of(y * yrows, 16)
    theirs = pl.multiple_of((1 - y) * yrows, 16)
    lo, hi = slice(0, part), slice(part, half)
    to_sib[0].wait_recv()
    pf[0:T, :] = pf[0:T, :] + pr[0:T, :].astype(F32)
    pm[0:T, :] = pf[0:T, :].astype(BF16)
    s2b0 = start(remote(pm.at[pl.ds(theirs, yrows), pl.ds(part, part)], r2b.at[pl.ds(0, yrows)], ypal))
    weights.wait_recv()
    wait_sib(0)
    pair_other = hidden_b(T, column(wrecv[0:1, :]), 1 - x)
    back_b(pair_other, T, 1 - c, put_send)
    start(to_sib[1])
    back_b(pair_other, T, c, put_keep)

    to_sib[1].wait_recv()
    pf[T:2 * T, :] = pf[T:2 * T, :] + pr[T:2 * T, :].astype(F32)
    pm[T:2 * T, :] = pf[T:2 * T, :].astype(BF16)
    s2a = start(remote(pm.at[pl.ds(T, T), pl.ds(0, part)], r2a, xpal))
    s2b1 = start(remote(pm.at[pl.ds(T + theirs, yrows), pl.ds(part, part)], r2b.at[pl.ds(yrows, yrows)], ypal))

    pass_y(1)
    in_rows.wait()
    wait_sib(1)
    out_rows = local(tok.at[1], rows_o)
    for i in range(2 * H // 256):
        units = slice(i * 256, i * 256 + 256)
        gt[units, :] = nt(wv[units, :], tok[1])

    s2a.wait_recv()
    s3a[...] = (pf[pl.ds(theirs, yrows), lo] + r2a[pl.ds(theirs, yrows), :].astype(F32)).astype(BF16)
    c3a = start(remote(s3a, r3a, ypal))
    s2b1.wait_recv()
    s3b[...] = (pf[pl.ds(T + mine, yrows), hi] + r2b[yrows:2 * yrows, :].astype(F32)).astype(BF16)
    c3b = start(remote(s3b, r3b, xpal))
    send_x(2)
    s2b0.wait_recv()
    qf[:, lo] = pf[pl.ds(mine, yrows), lo] + r2a[pl.ds(mine, yrows), :].astype(F32)
    qf[:, hi] = pf[pl.ds(mine, yrows), hi] + r2b[0:yrows, :].astype(F32)
    c3a.wait_recv()
    qf[:, lo] = qf[:, lo] + r3a[...].astype(F32)
    c3b.wait_recv()
    qf[:, hi] = qf[:, hi] + r3b[...].astype(F32)
    qs[...] = qf[...].astype(BF16)
    z_sums = []
    for k in range(1, zn):
        there = pl.ds(pl.multiple_of(((z + k) % zn) * zrows, 16), zrows)
        z_sums.append(start(remote(qs.at[there], r4.at[k - 1], zpal[k])))
    here = pl.multiple_of(z * zrows, 16)
    cols_me = pl.ds(pl.multiple_of(c * half, 128), half)
    chunk = qf[pl.ds(here, zrows), :] + tok[0, pl.ds(mine + here, zrows), cols_me].astype(F32)
    for k in range(1, zn):
        z_sums[k - 1].wait_recv()
        chunk = chunk + r4[k - 1].astype(F32)
    go[pl.ds(mine + here, zrows), cols_me] = chunk.astype(BF16)

    def finished(yy, k):
        return go.at[pl.ds(pl.multiple_of(yy * yrows + ((z + zn - k) % zn) * zrows, 16), zrows), cols_me]

    z_out = [None] + [start(remote(finished(y, 0), finished(y, 0), zpal[k])) for k in range(1, zn)]
    y_out, sib_out = [], []
    y_out.append(start(remote(finished(y, 0), finished(y, 0), ypal)))
    sib_out.append(start(remote(finished(y, 0), finished(y, 0), sib)))
    pass_x(2)
    for k in range(1, zn):
        z_out[k].wait_recv()
        y_out.append(start(remote(finished(y, k), finished(y, k), ypal)))
        sib_out.append(start(remote(finished(y, k), finished(y, k), sib)))
    pass_y(2)
    in_outs.wait()
    wait_sib(2)
    out_outs = local(tok.at[2], outs_o)
    scale_own = share(rc, pc, x)
    scale_c = jnp.concatenate([scale_own, wrecv[1:2, :]], axis=1)
    for i in range(H // 256):
        units = slice(i * 256, i * 256 + 256)
        uppers = slice(H + i * 256, H + i * 256 + 256)
        downs = slice(2 * H + i * 256, 2 * H + i * 256 + 256)
        act = nt(wv[downs, :], tok[2]) * scale_c
        upper = gt[uppers, :]
        activated, slope = silu_parts(gt[units, :])
        gt_o[units, :] = (act * upper * slope).astype(BF16)
        gt_o[uppers, :] = (act * activated).astype(BF16)
        gt_o[downs, :] = (activated * upper * scale_c).astype(BF16)
    for k in range(zn):
        y_out[k].wait_recv()
        sib_out.append(start(remote(finished(1 - y, k), finished(1 - y, k), sib)))
    for copy in sib_out:
        copy.wait_recv()
    out_go = local(go, gout)
    for copy in sent:
        copy.wait_send()
    out_rows.wait()
    out_outs.wait()
    out_go.wait()


def weight_kernel(parts, gt, rows, outs, gin, joint, last, gout, gtv, rowv, outv, ginv, jointv, lastv, sem):
    H, D = last.shape
    width = D // parts
    used = [0]

    def copy(src, dst):
        i = used[0]
        used[0] += 1
        made = pltpu.make_async_copy(src, dst, sem.at[i])
        made.start()
        return made

    first = copy(gt.at[pl.ds(0, 2 * H)], gtv.at[pl.ds(0, 2 * H)])
    spans = [pl.ds(j * width, width) for j in range(parts)]
    in_rows = [copy(rows.at[:, span], rowv.at[:, span]) for span in spans]
    second = copy(gt.at[pl.ds(2 * H, H)], gtv.at[pl.ds(2 * H, H)])
    in_outs = [copy(outs.at[:, span], outv.at[:, span]) for span in spans]
    in_gin = copy(gin, ginv)
    done = []
    first.wait()
    for j in range(parts):
        in_rows[j].wait()
        for i in range(2):
            units = pl.ds(i * H, H)
            jointv[units, spans[j]] = jnp.dot(
                gtv[units, :], rowv[:, spans[j]], preferred_element_type=F32
            ).astype(BF16)
            done.append(copy(jointv.at[units, spans[j]], joint.at[units, spans[j]]))
    in_gin.wait()
    done.append(copy(ginv, gout))
    second.wait()
    for j in range(parts):
        in_outs[j].wait()
        lastv[:, spans[j]] = jnp.dot(
            gtv[2 * H:3 * H, :], outv[:, spans[j]], preferred_element_type=F32
        ).astype(BF16)
        done.append(copy(lastv.at[:, spans[j]], last.at[:, spans[j]]))
    for made in done:
        made.wait()


def dense_body(
    grad_in, route_b, prob_b, pre_act, saved_in, grad_saved, route_c, prob_c, w_gate_up, w_down
):
    sections = lax.axis_size("segment")
    zn = sections // 4
    T, D = grad_in.shape
    H = w_down.shape[1]
    half, part = D // 2, D // 4
    copies = 24 + 1 + 2 + 3 + 2 + 2 * (zn - 1) + 3 * zn
    hbm = pl.BlockSpec(memory_space=pl.ANY)
    vmem = pl.BlockSpec(memory_space=pltpu.VMEM)
    gout, rows, outs, gt = pl.pallas_call(
        functools.partial(exchange_kernel, zn),
        out_shape=(
            jax.ShapeDtypeStruct((T, D), BF16),
            jax.ShapeDtypeStruct((2 * T, D), BF16),
            jax.ShapeDtypeStruct((2 * T, D), BF16),
            jax.ShapeDtypeStruct((3 * H, 2 * T), BF16),
        ),
        in_specs=[hbm] * 3 + [vmem] * 4 + [hbm] * 3,
        out_specs=(hbm, hbm, hbm, vmem),
        scratch_shapes=[
            pltpu.VMEM((3, 2 * T, D), BF16),
            pltpu.VMEM((3 * H, D), BF16),
            pltpu.VMEM((2, 2 * T, H), BF16),
            pltpu.VMEM((8, T), F32),
            pltpu.VMEM((8, T), F32),
            pltpu.VMEM((2 * T, half), BF16),
            pltpu.VMEM((2 * T, half), BF16),
            pltpu.VMEM((2 * T, half), F32),
            pltpu.VMEM((2 * T, half), BF16),
            pltpu.VMEM((T, part), BF16),
            pltpu.VMEM((T, part), BF16),
            pltpu.VMEM((T // 2, part), BF16),
            pltpu.VMEM((T // 2, part), BF16),
            pltpu.VMEM((T // 2, part), BF16),
            pltpu.VMEM((T // 2, part), BF16),
            pltpu.VMEM((T // 2, half), F32),
            pltpu.VMEM((T // 2, half), BF16),
            pltpu.VMEM((zn - 1, T // 2 // zn, half), BF16),
            pltpu.VMEM((T, D), BF16),
            pltpu.VMEM((2 * H, 2 * T), F32),
            pltpu.SemaphoreType.DMA((copies,)),
            pltpu.SemaphoreType.DMA((copies,)),
            pltpu.SemaphoreType.DMA((7 + 12,)),
        ],
        compiler_params=pltpu.CompilerParams(
            collective_id=0, has_side_effects=True, vmem_limit_bytes=56 * 1024 * 1024
        ),
        name="exchange",
    )(
        grad_in, saved_in, grad_saved, route_b.T, prob_b.T, route_c.T, prob_c.T,
        pre_act.reshape(2, 2 * T, H), w_gate_up.reshape(2 * H, D), w_down.reshape(H, D),
    )
    parts = 6
    joint, last, grad_out = pl.pallas_call(
        functools.partial(weight_kernel, parts),
        out_shape=(
            jax.ShapeDtypeStruct((2 * H, D), BF16),
            jax.ShapeDtypeStruct((H, D), BF16),
            jax.ShapeDtypeStruct((T, D), BF16),
        ),
        in_specs=[hbm] * 4,
        out_specs=(hbm,) * 3,
        scratch_shapes=[
            pltpu.VMEM((3 * H, 2 * T), BF16),
            pltpu.VMEM((2 * T, D), BF16),
            pltpu.VMEM((2 * T, D), BF16),
            pltpu.VMEM((T, D), BF16),
            pltpu.VMEM((2 * H, D), BF16),
            pltpu.VMEM((H, D), BF16),
            pltpu.SemaphoreType.DMA((5 * parts + 4,)),
        ],
        compiler_params=pltpu.CompilerParams(vmem_limit_bytes=63 * 1024 * 1024),
        name="weights",
    )(gt, rows, outs, gout)
    return grad_out, joint.reshape(1, 2, H, D), last.reshape(1, H, D)


def dense_fits(mesh):
    return mesh.shape["expert"] == 2 and mesh.shape["segment"] == 16


def solution(mesh):
    in_specs = (
        P("expert", None),
        P("expert", None),
        P("expert", None),
        P("expert", None, None, "segment"),
        P("expert", None),
        P("expert", None),
        P("expert", None),
        P("expert", None),
        P("expert", None, "segment", None),
        P("expert", "segment", None),
    )
    out_specs = (
        P("expert", None),
        P("expert", None, "segment", None),
        P("expert", "segment", None),
    )
    chosen = dense_body if dense_fits(mesh) else body
    return jax.shard_map(chosen, mesh=mesh, in_specs=in_specs, out_specs=out_specs, check_vma=False)
```
